32 devices in a mesh: expert: 16 (over z, x, core), tensor: 2 (over y).
Axes of the slice: x: 2, y: 2, z: 4, core: 2. Of those that a mesh axis runs over, the one named last changes fastest.
Arguments:
- tokens: bfloat16 [2048, 7168], P('expert', 'tensor'), may hold values from -6 to 6
- route_ids: int32 [2048, 8], P('expert'), may hold values from 0 to 255, as said below
- route_weight: float32 [2048, 8], P('expert'), may hold values from 0.1 to 2.5
- gate_up: bfloat16 [16, 2, 7168, 1024], P('expert', None, None, 'tensor'), may hold values from -0.0625 to 0.0625
- block_keep: int32 [16, 2, 112, 16], P('expert', None, None, 'tensor'), may hold values 0 or 1
Outputs:
- hidden_slots: bfloat16 [16, 128, 1024], P('expert', None, 'tensor')
The draws below stay inside these ranges and needn't reach their ends.
Inputs may be any that keep to these rules, and one draw needn't show every extreme that they name: `route_ids`: each row names 8 different experts. Within each aligned block of 128 rows no expert is named by more than 8 rows, and one expert numbered below 16 is named by exactly 8 rows in every block.
All inputs are finite; a program needn't handle non-finite values. No bound on the sum of `block_keep` on one device may be relied on, other than what follows from the above.
Results may differ from the reference program's by a relative error of at most 0.0051.
Values may be sent and summed in bfloat16 or wider, within the bound.
No kernel may reach another device: no remote copies, remote signals or barrier semaphores. Data moves between devices by JAX's collectives and lax.ppermute only.
A program may use at most 64 MiB of HBM per device.

```python
import jax
import jax.numpy as jnp
from jax import lax

D = 7168
EXPERTS = 256
TOP = 8
FF = 1024
BLOCK = 64
TOK_DEV = 128
CAP = 8
FLIGHT = 16
TOKENS = 2048
ROWS = 128


def draw_route_ids(key, part):
    block_count = TOKENS // TOK_DEV
    slot_total = EXPERTS * CAP
    popular_key = jax.random.fold_in(key, 11)
    hot_key = jax.random.fold_in(key, 12)
    favour = jax.random.randint(popular_key, (EXPERTS,), 0, 3).astype(jnp.int32)
    hottest = jax.random.randint(hot_key, (), 0, FLIGHT).astype(jnp.int32)
    expert_of_slot = jnp.arange(slot_total, dtype=jnp.int32) // CAP
    preference = favour[expert_of_slot] * 1024 + jnp.where(expert_of_slot == hottest, 8192, 0).astype(jnp.int32)

    def one_block(block_key):
        subkeys = jax.random.split(block_key, 3)
        jitter = jax.random.randint(subkeys[0], (slot_total,), 0, 4096).astype(jnp.int32)
        ranking = (jitter + preference) * slot_total + jnp.arange(slot_total, dtype=jnp.int32)
        chosen = jnp.argsort(-ranking)[:TOK_DEV * TOP]
        ordered = jnp.sort(expert_of_slot[chosen])
        layout_table = ordered.reshape(TOP, TOK_DEV).T
        layout_table = layout_table[jax.random.permutation(subkeys[1], TOK_DEV)]
        shuffle = jax.random.randint(subkeys[2], (TOK_DEV, TOP), 0, 1024).astype(jnp.int32) * TOP + jnp.arange(TOP, dtype=jnp.int32)[None, :]
        return jnp.take_along_axis(layout_table, jnp.argsort(shuffle, axis=1), axis=1)
    blocks = jax.vmap(one_block)(jax.random.split(key, block_count))
    return blocks.reshape(TOKENS, TOP).astype(jnp.int32)


def plant(values, rng, least, high):
    longest = values.shape.index(max(values.shape))
    spots = []
    for shift in (0, 1):
        where = [jax.random.randint(jax.random.fold_in(rng, axis), (), 0, length) for axis, length in enumerate(values.shape)]
        where[longest] = (where[longest] + shift) % values.shape[longest]
        spots.append(tuple(where))
    return values.at[spots[0]].set(least).at[spots[1]].set(high)


def steps_of(stream_key, dims, pieces, low, largest):
    factor_of = 1.0
    for position, parts in pieces:
        heights = jax.random.uniform(jax.random.fold_in(jax.random.fold_in(stream_key, 6), position), (parts,), jnp.float32, low / len(pieces), largest / len(pieces))
        factor_of = factor_of * jnp.repeat(jnp.exp(heights), dims[position] // parts).reshape((-1,) + (1,) * (len(dims) - 1 - position))
    return factor_of


def centred(rng, shape, deviation, most, cuts=(), kind=jnp.bfloat16):
    gain = steps_of(rng, shape, cuts, -0.22, 0.18) if cuts else 1.0
    values = jax.random.normal(rng, shape, jnp.float32) * deviation * gain
    return jnp.minimum(jnp.maximum(values, -most), most).astype(kind)


def setup_inputs(seed: int = 0) -> dict:
    key_list = jax.random.split(jax.random.key(seed), 6)
    tokens = centred(key_list[0], (TOKENS, D), 1.0, 6.0, ((0, 16), (1, 2)))
    route_ids = draw_route_ids(jax.random.fold_in(key_list[5], 71), 0)
    route_weight = jnp.clip(0.1 + 2.4 * jax.random.uniform(key_list[2], (TOKENS, TOP), jnp.float32) ** steps_of(key_list[2], (TOKENS, TOP), ((0, 16),), -0.2, 0.2), 0.1, 2.5)
    gate_up = centred(key_list[3], (FLIGHT, 2, D, FF), D ** -0.5, 0.0625, ((0, 16), (3, 2)))
    block_keep = plant((jax.random.randint(key_list[4], (FLIGHT, 2, D // BLOCK, FF // BLOCK), 0, 2) < 1).astype(jnp.int32), jax.random.fold_in(key_list[4], 1), 0, 1)
    return dict(tokens=tokens, route_ids=route_ids, route_weight=route_weight, gate_up=gate_up, block_keep=block_keep)


def expand_mask(keep_mask, block_size):
    widened = jnp.repeat(keep_mask, block_size, axis=1)
    return jnp.repeat(widened, block_size, axis=2)


def slot_table(picked, rounded, flight, capacity):
    token_count, pick_count = picked.shape
    flattened = picked.reshape(-1).astype(jnp.int32)
    matches = (flattened[:, None] == jnp.arange(flight, dtype=jnp.int32)[None, :]).astype(jnp.int32)
    before = (jnp.cumsum(matches, axis=0) - matches).astype(jnp.int32)
    slot_rank = jnp.sum(before * matches, axis=1).astype(jnp.int32)
    in_window = flattened < flight
    target = jnp.where(in_window, flattened * capacity + slot_rank, flight * capacity).astype(jnp.int32)
    source_row = (jnp.arange(token_count * pick_count, dtype=jnp.int32) // pick_count).astype(jnp.int32)
    token_of = jnp.full((flight * capacity,), -1, jnp.int32).at[target].set(source_row, mode="drop")
    weight_of = jnp.zeros((flight * capacity,), rounded.dtype).at[target].set(rounded.reshape(-1), mode="drop")
    return token_of, weight_of


def reference(tokens, route_ids, route_weight, gate_up, block_keep):
    flight = FLIGHT
    rounded = route_weight.astype(jnp.bfloat16)
    block_ids = route_ids.reshape(-1, TOK_DEV, TOP)
    block_weights = rounded.reshape(-1, TOK_DEV, TOP)
    token_of, weight_of = jax.vmap(lambda picked, scaling: slot_table(picked, scaling, flight, CAP))(block_ids, block_weights)
    block_count = block_ids.shape[0]
    offsets = (jnp.arange(block_count, dtype=jnp.int32) * TOK_DEV)[:, None]
    global_index = jnp.where(token_of >= 0, token_of + offsets, -1).astype(jnp.int32)
    global_index = global_index.reshape(block_count, flight, CAP).transpose(1, 0, 2).reshape(flight, ROWS)
    slot_weight = weight_of.reshape(block_count, flight, CAP).transpose(1, 0, 2).reshape(flight, ROWS)

    def one_expert(entries):
        source_index, scaling, matrices, keep_mask = entries
        filled = (source_index >= 0)[:, None]
        gathered = jnp.take(tokens, jnp.maximum(source_index, 0).astype(jnp.int32), axis=0)
        dispatched = jnp.where(filled, gathered, jnp.zeros((), tokens.dtype))
        masked = matrices * expand_mask(keep_mask, BLOCK).astype(matrices.dtype)
        gate_sums = jnp.dot(dispatched, masked[0], preferred_element_type=jnp.float32)
        up_sums = jnp.dot(dispatched, masked[1], preferred_element_type=jnp.float32)
        return (scaling.astype(jnp.float32)[:, None] * jax.nn.silu(gate_sums) * up_sums).astype(jnp.bfloat16)

    return lax.map(one_expert, (global_index, slot_weight, gate_up, block_keep))
```

```python
import functools

import jax
import jax.numpy as jnp
from jax import lax
from jax.experimental import pallas as pl
from jax.experimental.pallas import tpu as pltpu
from jax.sharding import PartitionSpec as P

BLOCK = 64
CAP = 8
LANES = 128
PAIR = 2 * CAP


def expand_mask(keep_mask, block_size):
    widened = jnp.repeat(keep_mask, block_size, axis=1)
    return jnp.repeat(widened, block_size, axis=2)


def slot_table(picked, rounded, flight, capacity):
    token_count, pick_count = picked.shape
    flattened = picked.reshape(-1)
    matches = (flattened[:, None] == jnp.arange(flight, dtype=jnp.int32)[None, :]).astype(jnp.int32)
    before = jnp.cumsum(matches, axis=0) - matches
    slot_rank = jnp.sum(before * matches, axis=1)
    in_window = flattened < flight
    target = jnp.where(in_window, flattened * capacity + slot_rank, flight * capacity)
    source_row = jnp.arange(token_count * pick_count, dtype=jnp.int32) // pick_count
    token_of = jnp.full((flight * capacity,), -1, jnp.int32).at[target].set(source_row, mode="drop")
    weight_of = (
        jnp.zeros((flight * capacity,), rounded.dtype)
        .at[target]
        .set(rounded.reshape(-1), mode="drop")
    )
    return (token_of, weight_of)


def activate(totals, scaling):
    factor = scaling.astype(jnp.float32)[..., None]
    return (factor * jax.nn.silu(totals[0]) * totals[1]).astype(jnp.bfloat16)


def gathered_form(tokens, route_ids, route_weight, gate_up, block_keep):
    flight = lax.axis_size("expert")
    masked = gate_up[0] * expand_mask(block_keep[0], BLOCK).astype(gate_up.dtype)
    hidden_units = masked.shape[2]
    rounded = route_weight.astype(jnp.bfloat16)
    token_of, weight_of = slot_table(route_ids, rounded, flight, CAP)
    filled = (token_of >= 0)[:, None]
    picked_rows = jnp.where(
        filled, jnp.take(tokens, jnp.maximum(token_of, 0), axis=0), jnp.zeros((), tokens.dtype)
    )
    outgoing = picked_rows.reshape(flight, CAP, tokens.shape[1])
    arrived = lax.all_to_all(outgoing, "expert", split_axis=0, concat_axis=0, tiled=True)
    scaling = lax.all_to_all(
        weight_of.reshape(flight, CAP), "expert", split_axis=0, concat_axis=0, tiled=True
    )
    arrived = lax.all_gather(arrived, "tensor", axis=2, tiled=True)
    totals = jnp.einsum("scd,kdf->kscf", arrived, masked, preferred_element_type=jnp.float32)
    return activate(totals, scaling).reshape(1, -1, hidden_units)


def chosen_rows(groups, place, block, ids, wgt):
    chip, core = place[0] // 2, lax.rem(place[0], 2)
    count = ids.shape[1]
    rows = lax.broadcasted_iota(jnp.int32, (count, count), 0)
    cols = lax.broadcasted_iota(jnp.int32, (count, count), 1)
    earlier = (rows < cols).astype(jnp.bfloat16)
    slot = lax.broadcasted_iota(jnp.int32, (PAIR, count), 0)
    rank_wanted = lax.rem(slot, CAP).astype(jnp.float32)
    here = slot // CAP == core ^ block
    rounded = wgt.astype(jnp.bfloat16).astype(jnp.float32)
    named, scale = [], []
    for k in range(groups):
        hit = ids == 2 * (chip ^ k) + core
        named.append(jnp.sum(hit.astype(jnp.float32), axis=0, keepdims=True))
        scale.append(jnp.sum(jnp.where(hit, rounded, 0.0), axis=0, keepdims=True))
    before = jnp.dot(
        jnp.concatenate(named, axis=0).astype(jnp.bfloat16), earlier, preferred_element_type=jnp.float32
    )
    chosen, weights = [], []
    for k in range(groups):
        pick = here & (named[k] > 0.5) & (before[k : k + 1] == rank_wanted)
        chosen.append(pick.astype(jnp.float32))
        weights.append(jnp.sum(chosen[k] * scale[k], axis=1, keepdims=True))
    return jnp.concatenate(chosen, axis=0).astype(jnp.bfloat16), jnp.concatenate(weights, axis=0)


def spans(width):
    step = next(s for s in (512, 384, 256, 128) if width % s == 0)
    return [slice(at, at + step) for at in range(0, width, step)]


def own_kernel(groups, place, ids_hbm, wgt_hbm, tok_hbm, out_ref, ids_ref, wgt_ref, tok_ref, sems):
    copies = [
        pltpu.make_async_copy(a, b, sems.at[i])
        for i, (a, b) in enumerate(((ids_hbm, ids_ref), (wgt_hbm, wgt_ref), (tok_hbm, tok_ref)))
    ]
    for copy in copies:
        copy.start()
    copies[0].wait()
    copies[1].wait()
    picks, weights = chosen_rows(groups, place, 0, ids_ref[...], wgt_ref[...])
    width = tok_ref.shape[1]
    copies[2].wait()
    for span in spans(width):
        got = jnp.dot(picks, tok_ref[:, span], preferred_element_type=jnp.float32)
        out_ref[:, span] = got.astype(out_ref.dtype)
    out_ref[:, width:] = jnp.broadcast_to(weights, (weights.shape[0], LANES)).astype(out_ref.dtype)


def pair_kernel(groups, near, place, ids_ref, wgt_ref, tok_ref, own_ref, near_ref, *far_refs):
    picks, weights = chosen_rows(groups, place, 1, ids_ref[...], wgt_ref[...])
    width = tok_ref.shape[1]

    def put(span, got):
        got = (got + own_ref[:, span].astype(jnp.float32)).astype(near_ref.dtype)
        near_ref[:, span] = got[: PAIR * near]
        for k, far_ref in enumerate(far_refs):
            far_ref[:, span] = got[PAIR * (near + k) : PAIR * (near + k + 1)]

    for span in spans(width):
        put(span, jnp.dot(picks, tok_ref[:, span], preferred_element_type=jnp.float32))
    put(slice(width, width + LANES), jnp.broadcast_to(weights, (weights.shape[0], LANES)))


def dispatch(place, ids, wgt, tok, partner, groups, near):
    count, width = tok.shape
    smem = pl.BlockSpec(memory_space=pltpu.SMEM)
    vmem = pl.BlockSpec(memory_space=pltpu.VMEM)
    hbm = pl.BlockSpec(memory_space=pl.ANY)
    cost = pl.CostEstimate(
        flops=2 * PAIR * groups * count * width, bytes_accessed=2 * count * width, transcendentals=0
    )
    own = pl.pallas_call(
        functools.partial(own_kernel, groups),
        out_shape=jax.ShapeDtypeStruct((PAIR * groups, width + LANES), tok.dtype),
        in_specs=[smem, hbm, hbm, hbm],
        out_specs=vmem,
        scratch_shapes=[pltpu.VMEM(a.shape, a.dtype) for a in (ids, wgt, tok)] + [pltpu.SemaphoreType.DMA((3,))],
        compiler_params=pltpu.CompilerParams(vmem_limit_bytes=16 << 20),
        cost_estimate=cost,
        name="own_rows",
    )(place, *(pltpu.with_memory_space_constraint(a, pltpu.HBM) for a in (ids, wgt, tok)))
    shapes = [jax.ShapeDtypeStruct((PAIR * near, width + LANES), tok.dtype)]
    shapes += [jax.ShapeDtypeStruct((PAIR, width + LANES), tok.dtype)] * (groups - near)
    return pl.pallas_call(
        functools.partial(pair_kernel, groups, near),
        out_shape=shapes,
        in_specs=[smem] + [vmem] * 4,
        out_specs=[vmem] * len(shapes),
        compiler_params=pltpu.CompilerParams(vmem_limit_bytes=16 << 20),
        cost_estimate=cost,
        name="pair_rows",
    )(place, *partner, own)


def mask_kernel(keep_ref, mat_hbm, out_ref, mask_ref, sems):
    parts = sems.shape[1]
    units, depth = out_ref.shape[2], out_ref.shape[1] // parts
    copies = [
        [
            pltpu.make_async_copy(
                mat_hbm.at[m, pl.ds(p * depth, depth)], out_ref.at[m, pl.ds(p * depth, depth)], sems.at[m, p]
            )
            for p in range(parts)
        ]
        for m in range(2)
    ]
    for p in range(parts):
        for m in range(2):
            copies[m][p].start()
    cols = keep_ref.shape[1]
    lane = lax.broadcasted_iota(jnp.int32, (cols, units), 1) // BLOCK
    row = lax.broadcasted_iota(jnp.int32, (cols, units), 0)
    widen = (lane == row).astype(jnp.bfloat16)
    for m in range(2):
        mask_ref[m] = lax.dot_general(
            keep_ref[m].astype(jnp.float32).astype(jnp.bfloat16),
            widen,
            (((0,), (0,)), ((), ())),
            preferred_element_type=jnp.float32,
        )
    for p in range(parts):
        for m in range(2):
            copies[m][p].wait()

            @pl.loop(0, depth // BLOCK)
            def _(r):
                at = p * (depth // BLOCK) + r
                keep = mask_ref[m, pl.ds(at, 1), :].astype(out_ref.dtype)
                span = pl.ds(pl.multiple_of(at * BLOCK, BLOCK), BLOCK)
                out_ref[m, span, :] = out_ref[m, span, :] * keep


def mask_matrices(keep, matrices):
    rows, units = matrices.shape[1:]
    parts = next(p for p in (14, 16, 8, 7, 4, 2, 1) if rows % (p * BLOCK) == 0)
    vmem = pl.BlockSpec(memory_space=pltpu.VMEM)
    return pl.pallas_call(
        mask_kernel,
        out_shape=jax.ShapeDtypeStruct(matrices.shape, matrices.dtype),
        in_specs=[vmem, pl.BlockSpec(memory_space=pl.ANY)],
        out_specs=vmem,
        scratch_shapes=[pltpu.VMEM((2, rows // BLOCK, units), jnp.float32), pltpu.SemaphoreType.DMA((2, parts))],
        compiler_params=pltpu.CompilerParams(vmem_limit_bytes=20 << 20),
        cost_estimate=pl.CostEstimate(flops=2 * rows * units, bytes_accessed=4 * rows * units, transcendentals=0),
        name="mask_matrices",
    )(keep, pltpu.with_memory_space_constraint(matrices, pltpu.HBM))


def join_kernel(near, own_ref, other_ref, *out_refs):
    for k, out_ref in enumerate(out_refs):
        span = slice(PAIR * (k + 1), PAIR * (k + 2))
        out_ref[:PAIR] = own_ref[span]
        out_ref[PAIR:] = other_ref[span]


def join(own, other, near):
    vmem = pl.BlockSpec(memory_space=pltpu.VMEM)
    return pl.pallas_call(
        functools.partial(join_kernel, near),
        out_shape=[jax.ShapeDtypeStruct((2 * PAIR, own.shape[1]), own.dtype)] * (near - 1),
        in_specs=[vmem] * 2,
        out_specs=[vmem] * (near - 1),
        compiler_params=pltpu.CompilerParams(vmem_limit_bytes=4 << 20),
        name="join",
    )(own, other)


def project_kernel(groups, near, last, place, mat_ref, *refs):
    pieces, refs = refs[:groups], refs[groups:]
    if last:
        total_ref, scale_ref, out_ref, x_ref = refs
    else:
        total_ref, scale_ref, x_ref = refs
    chip = place[0] // 2
    width = x_ref.shape[1]
    for k in range(groups):
        at = pl.multiple_of(PAIR * (chip ^ k), PAIR)
        half = slice(PAIR, None) if last and 0 < k < near else slice(0, PAIR)
        x_ref[pl.ds(at, PAIR), :] = pieces[k][half, :width]
        if not last:
            scale_ref[pl.ds(at, PAIR), :] = pieces[k][:PAIR, width:].astype(jnp.float32)
    share = 1 - place[1] if last else place[1]
    span = pl.ds(pl.multiple_of(share * width, BLOCK), width)
    totals = [jnp.dot(x_ref[...], mat_ref[m, span, :], preferred_element_type=jnp.float32) for m in range(2)]
    if last:
        gate, up = (total_ref[m] + totals[m] for m in range(2))
        out_ref[0] = (scale_ref[:, :1] * (gate / (1.0 + jnp.exp(-gate))) * up).astype(out_ref.dtype)
    else:
        for m in range(2):
            total_ref[m] = totals[m]


def project(place, matrices, pieces, groups, near, width, total=None, scale=None):
    last = total is not None
    units = matrices.shape[2]
    slots = PAIR * groups
    vmem = pl.BlockSpec(memory_space=pltpu.VMEM)
    args = [place, matrices, *pieces]
    if last:
        args += [total, scale]
        out_shape = jax.ShapeDtypeStruct((1, slots, units), jnp.bfloat16)
    else:
        out_shape = [
            jax.ShapeDtypeStruct((2, slots, units), jnp.float32),
            jax.ShapeDtypeStruct((slots, LANES), jnp.float32),
        ]
    return pl.pallas_call(
        functools.partial(project_kernel, groups, near, last),
        out_shape=out_shape,
        in_specs=[pl.BlockSpec(memory_space=pltpu.SMEM)] + [vmem] * (len(args) - 1),
        out_specs=vmem if last else [vmem, vmem],
        scratch_shapes=[pltpu.VMEM((slots, width), jnp.bfloat16)],
        compiler_params=pltpu.CompilerParams(vmem_limit_bytes=24 << 20),
        cost_estimate=pl.CostEstimate(
            flops=4 * slots * width * units, bytes_accessed=4 * width * units, transcendentals=slots * units
        ),
        name="project_last" if last else "project_first",
    )(*args)


def paired_form(tokens, route_ids, route_weight, gate_up, block_keep):
    n = lax.axis_size("expert")
    groups = n // 2
    near = groups // 2
    me = lax.axis_index("expert")
    place = jnp.stack([me, lax.axis_index("tensor")]).astype(jnp.int32)
    width = tokens.shape[1]

    def move(a, shift):
        return lax.ppermute(a, "expert", [(s, s ^ shift) for s in range(n)])

    def cross(a):
        return lax.ppermute(a, "tensor", [(0, 1), (1, 0)])

    ids, wgt = route_ids.T, route_weight.T
    partner = [move(a, 1) for a in (ids, wgt, tokens)]
    own, *far = dispatch(place, ids, wgt, tokens, partner, groups, near)
    keep = jnp.swapaxes(block_keep[0], 1, 2)
    keep, own = lax.optimization_barrier((keep, own))
    masked = mask_matrices(keep, gate_up[0])
    far_order = sorted(range(groups - near), key=lambda k: (k % 2, -k))
    far_in = [None] * (groups - near)
    for k in far_order:
        far_in[k] = move(far[k], 2 * (near + k))
    other, masked = lax.optimization_barrier((cross(own), masked))
    both = join(own, other, near)
    near_in = [move(b, 2 * (k + 1)) for k, b in enumerate(both)]
    far_other = [None] * (groups - near)
    for k in far_order:
        far_other[k] = cross(far_in[k])

    total, scale = project(place, masked, [own, *near_in, *far_in], groups, near, width)
    return project(place, masked, [other, *near_in, *far_other], groups, near, width, total, scale)


def solution(mesh):
    shares, experts = mesh.shape["tensor"], mesh.shape["expert"]
    paired = shares == 2 and 8 <= experts <= 16 and experts & (experts - 1) == 0
    return jax.shard_map(
        paired_form if paired else gathered_form,
        mesh=mesh,
        in_specs=(
            P("expert", "tensor"),
            P("expert", None),
            P("expert", None),
            P("expert", None, None, "tensor"),
            P("expert", None, None, "tensor"),
        ),
        out_specs=P("expert", None, "tensor"),
        check_vma=False,
    )
```

```python
import functools

import jax
import jax.numpy as jnp
from jax import lax
from jax.experimental import pallas as pl
from jax.experimental.pallas import tpu as pltpu
from jax.sharding import PartitionSpec as P

BLOCK = 64
CAP = 8
LANES = 128
PAIR = 2 * CAP
PIECES = 8


def expand_mask(keep_mask, block_size):
    widened = jnp.repeat(keep_mask, block_size, axis=1)
    return jnp.repeat(widened, block_size, axis=2)


def slot_table(picked, rounded, flight, capacity):
    token_count, pick_count = picked.shape
    flattened = picked.reshape(-1)
    matches = (flattened[:, None] == jnp.arange(flight, dtype=jnp.int32)[None, :]).astype(jnp.int32)
    before = jnp.cumsum(matches, axis=0) - matches
    slot_rank = jnp.sum(before * matches, axis=1)
    in_window = flattened < flight
    target = jnp.where(in_window, flattened * capacity + slot_rank, flight * capacity)
    source_row = jnp.arange(token_count * pick_count, dtype=jnp.int32) // pick_count
    token_of = jnp.full((flight * capacity,), -1, jnp.int32).at[target].set(source_row, mode="drop")
    weight_of = (
        jnp.zeros((flight * capacity,), rounded.dtype)
        .at[target]
        .set(rounded.reshape(-1), mode="drop")
    )
    return (token_of, weight_of)


def activate(totals, scaling):
    factor = scaling.astype(jnp.float32)[..., None]
    return (factor * jax.nn.silu(totals[0]) * totals[1]).astype(jnp.bfloat16)


def gathered_form(tokens, route_ids, route_weight, gate_up, block_keep):
    flight = lax.axis_size("expert")
    masked = gate_up[0] * expand_mask(block_keep[0], BLOCK).astype(gate_up.dtype)
    hidden_units = masked.shape[2]
    rounded = route_weight.astype(jnp.bfloat16)
    token_of, weight_of = slot_table(route_ids, rounded, flight, CAP)
    filled = (token_of >= 0)[:, None]
    picked_rows = jnp.where(
        filled, jnp.take(tokens, jnp.maximum(token_of, 0), axis=0), jnp.zeros((), tokens.dtype)
    )
    outgoing = picked_rows.reshape(flight, CAP, tokens.shape[1])
    arrived = lax.all_to_all(outgoing, "expert", split_axis=0, concat_axis=0, tiled=True)
    scaling = lax.all_to_all(
        weight_of.reshape(flight, CAP), "expert", split_axis=0, concat_axis=0, tiled=True
    )
    arrived = lax.all_gather(arrived, "tensor", axis=2, tiled=True)
    totals = jnp.einsum("scd,kdf->kscf", arrived, masked, preferred_element_type=jnp.float32)
    return activate(totals, scaling).reshape(1, -1, hidden_units)


def chosen_rows(groups, place, block, ids, wgt):
    chip, core = place[0] // 2, lax.rem(place[0], 2)
    count = ids.shape[1]
    rows = lax.broadcasted_iota(jnp.int32, (count, count), 0)
    cols = lax.broadcasted_iota(jnp.int32, (count, count), 1)
    earlier = (rows < cols).astype(jnp.bfloat16)
    slot = lax.broadcasted_iota(jnp.int32, (PAIR, count), 0)
    rank_wanted = lax.rem(slot, CAP).astype(jnp.float32)
    here = slot // CAP == core ^ block
    rounded = wgt.astype(jnp.bfloat16).astype(jnp.float32)
    named, scale = [], []
    for k in range(groups):
        hit = ids == 2 * (chip ^ k) + core
        named.append(jnp.sum(hit.astype(jnp.float32), axis=0, keepdims=True))
        scale.append(jnp.sum(jnp.where(hit, rounded, 0.0), axis=0, keepdims=True))
    before = jnp.dot(
        jnp.concatenate(named, axis=0).astype(jnp.bfloat16), earlier, preferred_element_type=jnp.float32
    )
    chosen, weights = [], []
    for k in range(groups):
        pick = here & (named[k] > 0.5) & (before[k : k + 1] == rank_wanted)
        chosen.append(pick.astype(jnp.float32))
        weights.append(jnp.sum(chosen[k] * scale[k], axis=1, keepdims=True))
    return jnp.concatenate(chosen, axis=0).astype(jnp.bfloat16), jnp.concatenate(weights, axis=0)


def spans(width):
    step = next(s for s in (512, 384, 256, 128) if width % s == 0)
    return [slice(at, at + step) for at in range(0, width, step)]


def own_kernel(groups, place, ids_hbm, wgt_hbm, tok_hbm, out_ref, ids_ref, wgt_ref, tok_ref, sems):
    copies = [
        pltpu.make_async_copy(a, b, sems.at[i])
        for i, (a, b) in enumerate(((ids_hbm, ids_ref), (wgt_hbm, wgt_ref), (tok_hbm, tok_ref)))
    ]
    for copy in copies:
        copy.start()
    copies[0].wait()
    copies[1].wait()
    picks, weights = chosen_rows(groups, place, 0, ids_ref[...], wgt_ref[...])
    width = tok_ref.shape[1]
    copies[2].wait()
    for span in spans(width):
        got = jnp.dot(picks, tok_ref[:, span], preferred_element_type=jnp.float32)
        out_ref[:, span] = got.astype(out_ref.dtype)
    out_ref[:, width:] = jnp.broadcast_to(weights, (weights.shape[0], LANES)).astype(out_ref.dtype)


def pair_kernel(groups, place, ids_ref, wgt_ref, tok_ref, own_ref, *out_refs):
    picks, weights = chosen_rows(groups, place, 1, ids_ref[...], wgt_ref[...])
    width = tok_ref.shape[1]

    def put(span, got):
        got = (got + own_ref[:, span].astype(jnp.float32)).astype(own_ref.dtype)
        for k, out_ref in enumerate(out_refs):
            out_ref[:, span] = got[PAIR * k : PAIR * (k + 1)]

    for span in spans(width):
        put(span, jnp.dot(picks, tok_ref[:, span], preferred_element_type=jnp.float32))
    put(slice(width, width + LANES), jnp.broadcast_to(weights, (weights.shape[0], LANES)))


def dispatch(place, ids, wgt, tok, partner, groups):
    count, width = tok.shape
    smem = pl.BlockSpec(memory_space=pltpu.SMEM)
    vmem = pl.BlockSpec(memory_space=pltpu.VMEM)
    hbm = pl.BlockSpec(memory_space=pl.ANY)
    cost = pl.CostEstimate(
        flops=2 * PAIR * groups * count * width, bytes_accessed=2 * count * width, transcendentals=0
    )
    own = pl.pallas_call(
        functools.partial(own_kernel, groups),
        out_shape=jax.ShapeDtypeStruct((PAIR * groups, width + LANES), tok.dtype),
        in_specs=[smem, hbm, hbm, hbm],
        out_specs=vmem,
        scratch_shapes=[pltpu.VMEM(a.shape, a.dtype) for a in (ids, wgt, tok)] + [pltpu.SemaphoreType.DMA((3,))],
        compiler_params=pltpu.CompilerParams(vmem_limit_bytes=16 << 20),
        cost_estimate=cost,
        name="own_rows",
    )(place, *(pltpu.with_memory_space_constraint(a, pltpu.HBM) for a in (ids, wgt, tok)))
    shapes = [jax.ShapeDtypeStruct((PAIR, width + LANES), tok.dtype)] * groups
    return pl.pallas_call(
        functools.partial(pair_kernel, groups),
        out_shape=shapes,
        in_specs=[smem] + [vmem] * 4,
        out_specs=[vmem] * len(shapes),
        compiler_params=pltpu.CompilerParams(vmem_limit_bytes=16 << 20),
        cost_estimate=cost,
        name="pair_rows",
    )(place, *partner, own)


def mask_kernel(m, keep_ref, mat_hbm, out_ref, mask_ref, sems):
    parts = sems.shape[0]
    units, depth = out_ref.shape[1], out_ref.shape[0] // parts
    copies = [
        pltpu.make_async_copy(
            mat_hbm.at[m, pl.ds(p * depth, depth)], out_ref.at[pl.ds(p * depth, depth)], sems.at[p]
        )
        for p in range(parts)
    ]
    for copy in copies:
        copy.start()
    cols = keep_ref.shape[1]
    lane = lax.broadcasted_iota(jnp.int32, (cols, units), 1) // BLOCK
    row = lax.broadcasted_iota(jnp.int32, (cols, units), 0)
    mask_ref[...] = lax.dot_general(
        keep_ref[m].astype(jnp.float32).astype(jnp.bfloat16),
        (lane == row).astype(jnp.bfloat16),
        (((0,), (0,)), ((), ())),
        preferred_element_type=jnp.float32,
    )
    for p, copy in enumerate(copies):
        copy.wait()

        @pl.loop(0, depth // BLOCK)
        def _(r):
            at = p * (depth // BLOCK) + r
            keep = mask_ref[pl.ds(at, 1), :].astype(out_ref.dtype)
            span = pl.ds(pl.multiple_of(at * BLOCK, BLOCK), BLOCK)
            out_ref[span, :] = out_ref[span, :] * keep


def mask_matrix(keep, matrices, m):
    rows, units = matrices.shape[1:]
    parts = next(p for p in (14, 16, 8, 7, 4, 2, 1) if rows % (p * BLOCK) == 0)
    vmem = pl.BlockSpec(memory_space=pltpu.VMEM)
    return pl.pallas_call(
        functools.partial(mask_kernel, m),
        out_shape=jax.ShapeDtypeStruct(matrices.shape[1:], matrices.dtype),
        in_specs=[vmem, pl.BlockSpec(memory_space=pl.ANY)],
        out_specs=vmem,
        scratch_shapes=[pltpu.VMEM((rows // BLOCK, units), jnp.float32), pltpu.SemaphoreType.DMA((parts,))],
        compiler_params=pltpu.CompilerParams(vmem_limit_bytes=10 << 20),
        cost_estimate=pl.CostEstimate(flops=8 * rows * units, bytes_accessed=8 * rows * units, transcendentals=0),
        name="mask_matrix",
    )(keep, pltpu.with_memory_space_constraint(matrices, pltpu.HBM))


def join_kernel(*refs):
    *piece_refs, out_ref = refs
    for k, piece_ref in enumerate(piece_refs):
        out_ref[PAIR * k : PAIR * (k + 1)] = piece_ref[...]


def join(*pieces):
    vmem = pl.BlockSpec(memory_space=pltpu.VMEM)
    return pl.pallas_call(
        join_kernel,
        out_shape=jax.ShapeDtypeStruct((PAIR * len(pieces), pieces[0].shape[1]), pieces[0].dtype),
        in_specs=[vmem] * len(pieces),
        out_specs=vmem,
        compiler_params=pltpu.CompilerParams(vmem_limit_bytes=4 << 20),
        name="join",
    )(*pieces)


def project_kernel(where, last, place, gate_ref, up_ref, *refs):
    count = 1 + max(i for i, _ in where)
    pieces, refs = refs[:count], refs[count:]
    if last:
        total_ref, scale_ref, out_ref, x_ref = refs
    else:
        total_ref, scale_ref, x_ref = refs
    chip = place[0] // 2
    width = x_ref.shape[1]
    for k, (i, row) in enumerate(where):
        at = pl.multiple_of(PAIR * (chip ^ k), PAIR)
        x_ref[pl.ds(at, PAIR), :] = pieces[i][row : row + PAIR, :width]
        if not last:
            scale_ref[pl.ds(at, PAIR), :] = pieces[i][row : row + PAIR, width:].astype(jnp.float32)
    share = 1 - place[1] if last else place[1]
    span = pl.ds(pl.multiple_of(share * width, BLOCK), width)
    totals = [jnp.dot(x_ref[...], ref[span, :], preferred_element_type=jnp.float32) for ref in (gate_ref, up_ref)]
    if last:
        gate, up = (total_ref[m] + totals[m] for m in range(2))
        out_ref[0] = (scale_ref[:, :1] * (gate / (1.0 + jnp.exp(-gate))) * up).astype(out_ref.dtype)
    else:
        for m in range(2):
            total_ref[m] = totals[m]


def project(place, matrices, pieces, where, width, total=None, scale=None):
    last = total is not None
    units = matrices[0].shape[1]
    slots = PAIR * len(where)
    vmem = pl.BlockSpec(memory_space=pltpu.VMEM)
    args = [place, *matrices, *pieces]
    if last:
        args += [total, scale]
        out_shape = jax.ShapeDtypeStruct((1, slots, units), jnp.bfloat16)
    else:
        out_shape = [
            jax.ShapeDtypeStruct((2, slots, units), jnp.float32),
            jax.ShapeDtypeStruct((slots, LANES), jnp.float32),
        ]
    return pl.pallas_call(
        functools.partial(project_kernel, where, last),
        out_shape=out_shape,
        in_specs=[pl.BlockSpec(memory_space=pltpu.SMEM)] + [vmem] * (len(args) - 1),
        out_specs=vmem if last else [vmem, vmem],
        scratch_shapes=[pltpu.VMEM((slots, width), jnp.bfloat16)],
        compiler_params=pltpu.CompilerParams(vmem_limit_bytes=24 << 20),
        cost_estimate=pl.CostEstimate(
            flops=4 * slots * width * units, bytes_accessed=4 * width * units, transcendentals=slots * units
        ),
        name="project_last" if last else "project_first",
    )(*args)


def paired_form(tokens, route_ids, route_weight, gate_up, block_keep):
    n = lax.axis_size("expert")
    groups = n // 2
    near = groups // 2
    me = lax.axis_index("expert")
    place = jnp.stack([me, lax.axis_index("tensor")]).astype(jnp.int32)
    width = tokens.shape[1]

    def move(a, shift):
        return lax.ppermute(a, "expert", [(s, s ^ shift) for s in range(n)])

    def cross(a):
        return lax.ppermute(a, "tensor", [(0, 1), (1, 0)])

    def after(a, *done):
        return lax.optimization_barrier((a, done))[0]

    ids, wgt = route_ids.T, route_weight.T
    partner = [move(a, 1) for a in (ids, wgt, tokens)]
    piece = list(dispatch(place, ids, wgt, tokens, partner, groups))
    keep = jnp.swapaxes(block_keep[0], 1, 2)
    got, other = [piece[0]] + [None] * (groups - 1), [None] * groups
    got[4] = move(piece[4], 8)
    got[6] = move(piece[6], 12)
    got[3] = move(piece[3], 6)
    got[2] = move(piece[2], 4)
    got[1] = move(piece[1], 2)
    up = mask_matrix(after(keep, piece[0]), gate_up[0], 1)
    got[7] = move(piece[7], 14)
    got[5] = move(piece[5], 10)
    gate = mask_matrix(after(keep, piece[0]), gate_up[0], 0)
    block1 = cross(got[3])
    block2 = cross(join(got[4], after(got[7], up)))
    block0 = cross(join(got[0], got[1], got[2]))
    block4 = cross(after(got[6], block1))
    block3 = cross(after(got[5], up, got[7]))
    masked = (gate, up)
    total, scale = project(place, masked, got, [(k, 0) for k in range(groups)], width)
    where = [(0, 0), (0, 16), (0, 32), (1, 0), (2, 0), (3, 0), (4, 0), (2, 16)]
    return project(place, masked, [block0, block1, block2, block3, block4], where, width, total, scale)


def solution(mesh):
    paired = mesh.shape["tensor"] == 2 and mesh.shape["expert"] == 2 * PIECES
    return jax.shard_map(
        paired_form if paired else gathered_form,
        mesh=mesh,
        in_specs=(
            P("expert", "tensor"),
            P("expert", None),
            P("expert", None),
            P("expert", None, None, "tensor"),
            P("expert", None, None, "tensor"),
        ),
        out_specs=P("expert", None, "tensor"),
        check_vma=False,
    )
```

```python
import functools

import jax
import jax.numpy as jnp
from jax import lax
from jax.experimental import pallas as pl
from jax.experimental.pallas import tpu as pltpu
from jax.sharding import PartitionSpec as P

BLOCK = 64
CAP = 8
LANES = 128
PAIR = 2 * CAP
PIECES = 8


def expand_mask(keep_mask, block_size):
    widened = jnp.repeat(keep_mask, block_size, axis=1)
    return jnp.repeat(widened, block_size, axis=2)


def slot_table(picked, rounded, flight, capacity):
    token_count, pick_count = picked.shape
    flattened = picked.reshape(-1)
    matches = (flattened[:, None] == jnp.arange(flight, dtype=jnp.int32)[None, :]).astype(jnp.int32)
    before = jnp.cumsum(matches, axis=0) - matches
    slot_rank = jnp.sum(before * matches, axis=1)
    in_window = flattened < flight
    target = jnp.where(in_window, flattened * capacity + slot_rank, flight * capacity)
    source_row = jnp.arange(token_count * pick_count, dtype=jnp.int32) // pick_count
    token_of = jnp.full((flight * capacity,), -1, jnp.int32).at[target].set(source_row, mode="drop")
    weight_of = (
        jnp.zeros((flight * capacity,), rounded.dtype)
        .at[target]
        .set(rounded.reshape(-1), mode="drop")
    )
    return (token_of, weight_of)


def activate(totals, scaling):
    factor = scaling.astype(jnp.float32)[..., None]
    return (factor * jax.nn.silu(totals[0]) * totals[1]).astype(jnp.bfloat16)


def gathered_form(tokens, route_ids, route_weight, gate_up, block_keep):
    flight = lax.axis_size("expert")
    masked = gate_up[0] * expand_mask(block_keep[0], BLOCK).astype(gate_up.dtype)
    hidden_units = masked.shape[2]
    rounded = route_weight.astype(jnp.bfloat16)
    token_of, weight_of = slot_table(route_ids, rounded, flight, CAP)
    filled = (token_of >= 0)[:, None]
    picked_rows = jnp.where(
        filled, jnp.take(tokens, jnp.maximum(token_of, 0), axis=0), jnp.zeros((), tokens.dtype)
    )
    outgoing = picked_rows.reshape(flight, CAP, tokens.shape[1])
    arrived = lax.all_to_all(outgoing, "expert", split_axis=0, concat_axis=0, tiled=True)
    scaling = lax.all_to_all(
        weight_of.reshape(flight, CAP), "expert", split_axis=0, concat_axis=0, tiled=True
    )
    arrived = lax.all_gather(arrived, "tensor", axis=2, tiled=True)
    totals = jnp.einsum("scd,kdf->kscf", arrived, masked, preferred_element_type=jnp.float32)
    return activate(totals, scaling).reshape(1, -1, hidden_units)


def chosen_rows(groups, place, block, ids, wgt):
    chip, core = place[0] // 2, lax.rem(place[0], 2)
    count = ids.shape[1]
    rows = lax.broadcasted_iota(jnp.int32, (count, count), 0)
    cols = lax.broadcasted_iota(jnp.int32, (count, count), 1)
    earlier = (rows < cols).astype(jnp.bfloat16)
    slot = lax.broadcasted_iota(jnp.int32, (PAIR, count), 0)
    rank_wanted = lax.rem(slot, CAP).astype(jnp.float32)
    here = slot // CAP == core ^ block
    rounded = wgt.astype(jnp.bfloat16).astype(jnp.float32)
    named, scale = [], []
    for k in range(groups):
        hit = ids == 2 * (chip ^ k) + core
        named.append(jnp.sum(hit.astype(jnp.float32), axis=0, keepdims=True))
        scale.append(jnp.sum(jnp.where(hit, rounded, 0.0), axis=0, keepdims=True))
    before = jnp.dot(
        jnp.concatenate(named, axis=0).astype(jnp.bfloat16), earlier, preferred_element_type=jnp.float32
    )
    chosen, weights = [], []
    for k in range(groups):
        pick = here & (named[k] > 0.5) & (before[k : k + 1] == rank_wanted)
        chosen.append(pick.astype(jnp.float32))
        weights.append(jnp.sum(chosen[k] * scale[k], axis=1, keepdims=True))
    return jnp.concatenate(chosen, axis=0).astype(jnp.bfloat16), jnp.concatenate(weights, axis=0)


def spans(width):
    step = next(s for s in (512, 384, 256, 128) if width % s == 0)
    return [slice(at, at + step) for at in range(0, width, step)]


def own_kernel(groups, place, ids_hbm, wgt_hbm, tok_hbm, out_ref, ids_ref, wgt_ref, tok_ref, sems):
    copies = [
        pltpu.make_async_copy(a, b, sems.at[i])
        for i, (a, b) in enumerate(((ids_hbm, ids_ref), (wgt_hbm, wgt_ref), (tok_hbm, tok_ref)))
    ]
    for copy in copies:
        copy.start()
    copies[0].wait()
    copies[1].wait()
    picks, weights = chosen_rows(groups, place, 0, ids_ref[...], wgt_ref[...])
    width = tok_ref.shape[1]
    copies[2].wait()
    for span in spans(width):
        got = jnp.dot(picks, tok_ref[:, span], preferred_element_type=jnp.float32)
        out_ref[:, span] = got.astype(out_ref.dtype)
    out_ref[:, width:] = jnp.broadcast_to(weights, (weights.shape[0], LANES)).astype(out_ref.dtype)


def pair_kernel(groups, place, ids_ref, wgt_ref, tok_ref, own_ref, *out_refs):
    picks, weights = chosen_rows(groups, place, 1, ids_ref[...], wgt_ref[...])
    width = tok_ref.shape[1]

    def put(span, got):
        got = (got + own_ref[:, span].astype(jnp.float32)).astype(own_ref.dtype)
        for k, out_ref in enumerate(out_refs):
            out_ref[:, span] = got[PAIR * k : PAIR * (k + 1)]

    for span in spans(width):
        put(span, jnp.dot(picks, tok_ref[:, span], preferred_element_type=jnp.float32))
    put(slice(width, width + LANES), jnp.broadcast_to(weights, (weights.shape[0], LANES)))


def dispatch(place, ids, wgt, tok, partner, groups):
    count, width = tok.shape
    smem = pl.BlockSpec(memory_space=pltpu.SMEM)
    vmem = pl.BlockSpec(memory_space=pltpu.VMEM)
    hbm = pl.BlockSpec(memory_space=pl.ANY)
    cost = pl.CostEstimate(
        flops=2 * PAIR * groups * count * width, bytes_accessed=2 * count * width, transcendentals=0
    )
    own = pl.pallas_call(
        functools.partial(own_kernel, groups),
        out_shape=jax.ShapeDtypeStruct((PAIR * groups, width + LANES), tok.dtype),
        in_specs=[smem, hbm, hbm, hbm],
        out_specs=vmem,
        scratch_shapes=[pltpu.VMEM(a.shape, a.dtype) for a in (ids, wgt, tok)] + [pltpu.SemaphoreType.DMA((3,))],
        compiler_params=pltpu.CompilerParams(vmem_limit_bytes=16 << 20),
        cost_estimate=cost,
        name="own_rows",
    )(place, *(pltpu.with_memory_space_constraint(a, pltpu.HBM) for a in (ids, wgt, tok)))
    shapes = [jax.ShapeDtypeStruct((PAIR, width + LANES), tok.dtype)] * groups
    return pl.pallas_call(
        functools.partial(pair_kernel, groups),
        out_shape=shapes,
        in_specs=[smem] + [vmem] * 4,
        out_specs=[vmem] * len(shapes),
        compiler_params=pltpu.CompilerParams(vmem_limit_bytes=16 << 20),
        cost_estimate=cost,
        name="pair_rows",
    )(place, *partner, own)


def mask_kernel(m, keep_hbm, mat_hbm, out_ref, keep_ref, mask_ref, sems):
    parts = sems.shape[0] - 1
    units, depth = out_ref.shape[1], out_ref.shape[0] // parts
    fetch_keep = pltpu.make_async_copy(keep_hbm.at[m], keep_ref, sems.at[parts])
    fetch_keep.start()
    copies = [
        pltpu.make_async_copy(
            mat_hbm.at[m, pl.ds(p * depth, depth)], out_ref.at[pl.ds(p * depth, depth)], sems.at[p]
        )
        for p in range(parts)
    ]
    for copy in copies:
        copy.start()
    cols = keep_ref.shape[0]
    lane = lax.broadcasted_iota(jnp.int32, (cols, units), 1) // BLOCK
    row = lax.broadcasted_iota(jnp.int32, (cols, units), 0)
    fetch_keep.wait()
    mask_ref[...] = lax.dot_general(
        keep_ref[...].astype(jnp.float32).astype(jnp.bfloat16),
        (lane == row).astype(jnp.bfloat16),
        (((0,), (0,)), ((), ())),
        preferred_element_type=jnp.float32,
    )
    for p, copy in enumerate(copies):
        copy.wait()

        @pl.loop(0, depth // BLOCK)
        def _(r):
            at = p * (depth // BLOCK) + r
            keep = mask_ref[pl.ds(at, 1), :].astype(out_ref.dtype)
            span = pl.ds(pl.multiple_of(at * BLOCK, BLOCK), BLOCK)
            out_ref[span, :] = out_ref[span, :] * keep


def mask_matrix(keep, matrices, m, cost=0):
    rows, units = matrices.shape[1:]
    parts = next(p for p in (14, 16, 8, 7, 4, 2, 1) if rows % (p * BLOCK) == 0)
    hbm = pl.BlockSpec(memory_space=pl.ANY)
    return pl.pallas_call(
        functools.partial(mask_kernel, m),
        out_shape=jax.ShapeDtypeStruct(matrices.shape[1:], matrices.dtype),
        in_specs=[hbm, hbm],
        out_specs=pl.BlockSpec(memory_space=pltpu.VMEM),
        scratch_shapes=[
            pltpu.VMEM(keep.shape[1:], keep.dtype),
            pltpu.VMEM((rows // BLOCK, units), jnp.float32),
            pltpu.SemaphoreType.DMA((parts + 1,)),
        ],
        compiler_params=pltpu.CompilerParams(vmem_limit_bytes=10 << 20),
        cost_estimate=pl.CostEstimate(flops=0, bytes_accessed=cost, transcendentals=0),
        name="mask_matrix",
    )(*(pltpu.with_memory_space_constraint(a, pltpu.HBM) for a in (keep, matrices)))


def join_kernel(starts, *refs):
    *piece_refs, out_ref = refs
    width = out_ref.shape[1]
    for k, (start, piece_ref) in enumerate(zip(starts, piece_refs)):
        have = min(width, piece_ref.shape[1])
        out_ref[PAIR * k : PAIR * (k + 1), :have] = piece_ref[start : start + PAIR, :have]
        if have < width:
            out_ref[PAIR * k : PAIR * (k + 1), have:] = jnp.zeros((PAIR, width - have), out_ref.dtype)


def join(width, *pieces, cost=0):
    pieces = [p if isinstance(p, tuple) else (p, 0) for p in pieces]
    vmem = pl.BlockSpec(memory_space=pltpu.VMEM)
    return pl.pallas_call(
        functools.partial(join_kernel, [start for _, start in pieces]),
        out_shape=jax.ShapeDtypeStruct((PAIR * len(pieces), width), pieces[0][0].dtype),
        in_specs=[vmem] * len(pieces),
        out_specs=vmem,
        compiler_params=pltpu.CompilerParams(vmem_limit_bytes=4 << 20),
        cost_estimate=pl.CostEstimate(flops=0, bytes_accessed=cost, transcendentals=0),
        name="join",
    )(*(array for array, _ in pieces))


def project_kernel(where, last, place, gate_ref, up_ref, *refs):
    count = 1 + max(i for i, _ in where)
    pieces, refs = refs[:count], refs[count:]
    if last:
        total_ref, scale_ref, out_ref, x_ref = refs
    else:
        total_ref, scale_ref, x_ref = refs
    chip = place[0] // 2
    width = x_ref.shape[1]
    for k, (i, row) in enumerate(where):
        at = pl.multiple_of(PAIR * (chip ^ k), PAIR)
        x_ref[pl.ds(at, PAIR), :] = pieces[i][row : row + PAIR, :width]
        if not last:
            scale_ref[pl.ds(at, PAIR), :] = pieces[i][row : row + PAIR, width:].astype(jnp.float32)
    share = 1 - place[1] if last else place[1]
    span = pl.ds(pl.multiple_of(share * width, BLOCK), width)
    totals = [jnp.dot(x_ref[...], ref[span, :], preferred_element_type=jnp.float32) for ref in (gate_ref, up_ref)]
    if last:
        gate, up = (total_ref[m] + totals[m] for m in range(2))
        out_ref[0] = (scale_ref[:, :1] * (gate / (1.0 + jnp.exp(-gate))) * up).astype(out_ref.dtype)
    else:
        for m in range(2):
            total_ref[m] = totals[m]


def project(place, matrices, pieces, where, width, total=None, scale=None):
    last = total is not None
    units = matrices[0].shape[1]
    slots = PAIR * len(where)
    vmem = pl.BlockSpec(memory_space=pltpu.VMEM)
    args = [place, *matrices, *pieces]
    if last:
        args += [total, scale]
        out_shape = jax.ShapeDtypeStruct((1, slots, units), jnp.bfloat16)
    else:
        out_shape = [
            jax.ShapeDtypeStruct((2, slots, units), jnp.float32),
            jax.ShapeDtypeStruct((slots, LANES), jnp.float32),
        ]
    return pl.pallas_call(
        functools.partial(project_kernel, where, last),
        out_shape=out_shape,
        in_specs=[pl.BlockSpec(memory_space=pltpu.SMEM)] + [vmem] * (len(args) - 1),
        out_specs=vmem if last else [vmem, vmem],
        scratch_shapes=[pltpu.VMEM((slots, width), jnp.bfloat16)],
        compiler_params=pltpu.CompilerParams(vmem_limit_bytes=24 << 20),
        cost_estimate=pl.CostEstimate(
            flops=4 * slots * width * units, bytes_accessed=4 * width * units, transcendentals=slots * units
        ),
        name="project_last" if last else "project_first",
    )(*args)


def paired_form(tokens, route_ids, route_weight, gate_up, block_keep):
    n = lax.axis_size("expert")
    groups = n // 2
    me = lax.axis_index("expert")
    place = jnp.stack([me, lax.axis_index("tensor")]).astype(jnp.int32)
    width = tokens.shape[1]

    def move(a, shift):
        return lax.ppermute(a, "expert", [(s, s ^ shift) for s in range(n)])

    def cross(a):
        return lax.ppermute(a, "tensor", [(0, 1), (1, 0)])

    def after(a, *done):
        return lax.optimization_barrier((a, done))[0]

    ids, wgt = route_ids.T, route_weight.T
    partner = [move(a, 1) for a in (ids, wgt, tokens)]
    piece = list(dispatch(place, ids, wgt, tokens, partner, groups))
    keep = jnp.swapaxes(block_keep[0], 1, 2)
    got = [piece[0]] + [None] * (groups - 1)
    got[1] = move(piece[1], 2)
    block0 = cross(join(width, got[0], piece[2], cost=10 << 20))
    got[3] = move(piece[3], 6)
    got[7] = move(piece[7], 14)
    got[4] = move(piece[4], 8)
    got[2] = move(join(width + LANES, piece[2], (block0, 16), cost=10 << 20), 4)
    gate = mask_matrix(after(keep, piece[0], got[1]), gate_up[0], 0, cost=30 << 20)
    got[6] = move(after(piece[6], got[3]), 12)
    block4 = cross(join(width, got[6], cost=10 << 20))
    block1 = cross(join(width, got[1], got[3]))
    got[5] = move(after(piece[5], got[4]), 10)
    block2 = cross(join(width, got[4], got[7], cost=10 << 20))
    up = mask_matrix(after(keep, piece[0], got[4]), gate_up[0], 1, cost=30 << 20)
    block3 = cross(join(width, after(got[5], up), cost=10 << 20))
    masked = (gate, up)
    total, scale = project(place, masked, got, [(k, 0) for k in range(groups)], width)
    where = [(0, 0), (1, 0), (5, 16), (1, 16), (2, 0), (3, 0), (4, 0), (2, 16)]
    return project(place, masked, [block0, block1, block2, block3, block4, got[2]], where, width, total, scale)


def solution(mesh):
    paired = mesh.shape["tensor"] == 2 and mesh.shape["expert"] == 2 * PIECES
    return jax.shard_map(
        paired_form if paired else gathered_form,
        mesh=mesh,
        in_specs=(
            P("expert", "tensor"),
            P("expert", None),
            P("expert", None),
            P("expert", None, None, "tensor"),
            P("expert", None, None, "tensor"),
        ),
        out_specs=P("expert", None, "tensor"),
        check_vma=False,
    )
```

```python
import functools

import jax
import jax.numpy as jnp
from jax import lax
from jax.experimental import pallas as pl
from jax.experimental.pallas import tpu as pltpu
from jax.sharding import PartitionSpec as P

BLOCK = 64
CAP = 8
LANES = 128
PAIR = 2 * CAP
PIECES = 8


def expand_mask(keep_mask, block_size):
    widened = jnp.repeat(keep_mask, block_size, axis=1)
    return jnp.repeat(widened, block_size, axis=2)


def slot_table(picked, rounded, flight, capacity):
    token_count, pick_count = picked.shape
    flattened = picked.reshape(-1)
    matches = (flattened[:, None] == jnp.arange(flight, dtype=jnp.int32)[None, :]).astype(jnp.int32)
    before = jnp.cumsum(matches, axis=0) - matches
    slot_rank = jnp.sum(before * matches, axis=1)
    in_window = flattened < flight
    target = jnp.where(in_window, flattened * capacity + slot_rank, flight * capacity)
    source_row = jnp.arange(token_count * pick_count, dtype=jnp.int32) // pick_count
    token_of = jnp.full((flight * capacity,), -1, jnp.int32).at[target].set(source_row, mode="drop")
    weight_of = (
        jnp.zeros((flight * capacity,), rounded.dtype)
        .at[target]
        .set(rounded.reshape(-1), mode="drop")
    )
    return (token_of, weight_of)


def activate(totals, scaling):
    factor = scaling.astype(jnp.float32)[..., None]
    return (factor * jax.nn.silu(totals[0]) * totals[1]).astype(jnp.bfloat16)


def gathered_form(tokens, route_ids, route_weight, gate_up, block_keep):
    flight = lax.axis_size("expert")
    masked = gate_up[0] * expand_mask(block_keep[0], BLOCK).astype(gate_up.dtype)
    hidden_units = masked.shape[2]
    rounded = route_weight.astype(jnp.bfloat16)
    token_of, weight_of = slot_table(route_ids, rounded, flight, CAP)
    filled = (token_of >= 0)[:, None]
    picked_rows = jnp.where(
        filled, jnp.take(tokens, jnp.maximum(token_of, 0), axis=0), jnp.zeros((), tokens.dtype)
    )
    outgoing = picked_rows.reshape(flight, CAP, tokens.shape[1])
    arrived = lax.all_to_all(outgoing, "expert", split_axis=0, concat_axis=0, tiled=True)
    scaling = lax.all_to_all(
        weight_of.reshape(flight, CAP), "expert", split_axis=0, concat_axis=0, tiled=True
    )
    arrived = lax.all_gather(arrived, "tensor", axis=2, tiled=True)
    totals = jnp.einsum("scd,kdf->kscf", arrived, masked, preferred_element_type=jnp.float32)
    return activate(totals, scaling).reshape(1, -1, hidden_units)


def chosen_rows(groups, place, block, ids, wgt):
    chip, core = place[0] // 2, lax.rem(place[0], 2)
    count = ids.shape[1]
    rows = lax.broadcasted_iota(jnp.int32, (count, count), 0)
    cols = lax.broadcasted_iota(jnp.int32, (count, count), 1)
    earlier = (rows < cols).astype(jnp.bfloat16)
    slot = lax.broadcasted_iota(jnp.int32, (PAIR, count), 0)
    rank_wanted = lax.rem(slot, CAP).astype(jnp.float32)
    here = slot // CAP == core ^ block
    rounded = wgt.astype(jnp.bfloat16).astype(jnp.float32)
    named, scale = [], []
    for k in range(groups):
        hit = ids == 2 * (chip ^ k) + core
        named.append(jnp.sum(hit.astype(jnp.float32), axis=0, keepdims=True))
        scale.append(jnp.sum(jnp.where(hit, rounded, 0.0), axis=0, keepdims=True))
    before = jnp.dot(
        jnp.concatenate(named, axis=0).astype(jnp.bfloat16), earlier, preferred_element_type=jnp.float32
    )
    chosen, weights = [], []
    for k in range(groups):
        pick = here & (named[k] > 0.5) & (before[k : k + 1] == rank_wanted)
        chosen.append(pick.astype(jnp.float32))
        weights.append(jnp.sum(chosen[k] * scale[k], axis=1, keepdims=True))
    return jnp.concatenate(chosen, axis=0).astype(jnp.bfloat16), jnp.concatenate(weights, axis=0)


def spans(width):
    step = next(s for s in (512, 384, 256, 128) if width % s == 0)
    return [slice(at, at + step) for at in range(0, width, step)]


def own_kernel(groups, place, ids_hbm, wgt_hbm, tok_hbm, out_ref, ids_ref, wgt_ref, tok_ref, sems):
    count = tok_ref.shape[0]
    part = count // (sems.shape[0] - 2)
    pairs = [(ids_hbm, ids_ref), (wgt_hbm, wgt_ref)]
    pairs += [(tok_hbm.at[pl.ds(at, part)], tok_ref.at[pl.ds(at, part)]) for at in range(0, count, part)]
    copies = [pltpu.make_async_copy(a, b, sems.at[i]) for i, (a, b) in enumerate(pairs)]
    for copy in copies:
        copy.start()
    copies[0].wait()
    copies[1].wait()
    picks, weights = chosen_rows(groups, place, 0, ids_ref[...], wgt_ref[...])
    width = tok_ref.shape[1]
    for copy in copies[2:]:
        copy.wait()
    for span in spans(width):
        got = jnp.dot(picks, tok_ref[:, span], preferred_element_type=jnp.float32)
        out_ref[:, span] = got.astype(out_ref.dtype)
    out_ref[:, width:] = jnp.broadcast_to(weights, (weights.shape[0], LANES)).astype(out_ref.dtype)


def pair_kernel(groups, place, ids_ref, wgt_ref, tok_ref, own_ref, *out_refs):
    picks, weights = chosen_rows(groups, place, 1, ids_ref[...], wgt_ref[...])
    width = tok_ref.shape[1]

    def put(span, got):
        got = (got + own_ref[:, span].astype(jnp.float32)).astype(own_ref.dtype)
        for k, out_ref in enumerate(out_refs):
            out_ref[:, span] = got[PAIR * k : PAIR * (k + 1)]

    for span in spans(width):
        put(span, jnp.dot(picks, tok_ref[:, span], preferred_element_type=jnp.float32))
    put(slice(width, width + LANES), jnp.broadcast_to(weights, (weights.shape[0], LANES)))


def dispatch(place, ids, wgt, tok, partner, groups):
    count, width = tok.shape
    smem = pl.BlockSpec(memory_space=pltpu.SMEM)
    vmem = pl.BlockSpec(memory_space=pltpu.VMEM)
    hbm = pl.BlockSpec(memory_space=pl.ANY)
    cost = pl.CostEstimate(
        flops=2 * PAIR * groups * count * width, bytes_accessed=2 * count * width, transcendentals=0
    )
    own = pl.pallas_call(
        functools.partial(own_kernel, groups),
        out_shape=jax.ShapeDtypeStruct((PAIR * groups, width + LANES), tok.dtype),
        in_specs=[smem, hbm, hbm, hbm],
        out_specs=vmem,
        scratch_shapes=[pltpu.VMEM(a.shape, a.dtype) for a in (ids, wgt, tok)] + [pltpu.SemaphoreType.DMA((2 + (4 if count % 64 == 0 else 1),))],
        compiler_params=pltpu.CompilerParams(vmem_limit_bytes=16 << 20),
        cost_estimate=cost,
        name="own_rows",
    )(place, *(pltpu.with_memory_space_constraint(a, pltpu.HBM) for a in (ids, wgt, tok)))
    shapes = [jax.ShapeDtypeStruct((PAIR, width + LANES), tok.dtype)] * groups
    return pl.pallas_call(
        functools.partial(pair_kernel, groups),
        out_shape=shapes,
        in_specs=[smem] + [vmem] * 4,
        out_specs=[vmem] * len(shapes),
        compiler_params=pltpu.CompilerParams(vmem_limit_bytes=16 << 20),
        cost_estimate=cost,
        name="pair_rows",
    )(place, *partner, own)


def mask_kernel(m, keep_hbm, mat_hbm, out_ref, keep_ref, mask_ref, sems):
    parts = sems.shape[0] - 1
    units, depth = out_ref.shape[1], out_ref.shape[0] // parts
    fetch_keep = pltpu.make_async_copy(keep_hbm.at[m], keep_ref, sems.at[parts])
    fetch_keep.start()
    copies = [
        pltpu.make_async_copy(
            mat_hbm.at[m, pl.ds(p * depth, depth)], out_ref.at[pl.ds(p * depth, depth)], sems.at[p]
        )
        for p in range(parts)
    ]
    for copy in copies:
        copy.start()
    cols = keep_ref.shape[0]
    lane = lax.broadcasted_iota(jnp.int32, (cols, units), 1) // BLOCK
    row = lax.broadcasted_iota(jnp.int32, (cols, units), 0)
    fetch_keep.wait()
    mask_ref[...] = lax.dot_general(
        keep_ref[...].astype(jnp.float32).astype(jnp.bfloat16),
        (lane == row).astype(jnp.bfloat16),
        (((0,), (0,)), ((), ())),
        preferred_element_type=jnp.float32,
    )
    for p, copy in enumerate(copies):
        copy.wait()

        @pl.loop(0, depth // BLOCK)
        def _(r):
            at = p * (depth // BLOCK) + r
            keep = mask_ref[pl.ds(at, 1), :].astype(out_ref.dtype)
            span = pl.ds(pl.multiple_of(at * BLOCK, BLOCK), BLOCK)
            out_ref[span, :] = out_ref[span, :] * keep


def mask_matrix(keep, matrices, m, cost=0):
    rows, units = matrices.shape[1:]
    parts = next(p for p in (14, 16, 8, 7, 4, 2, 1) if rows % (p * BLOCK) == 0)
    hbm = pl.BlockSpec(memory_space=pl.ANY)
    return pl.pallas_call(
        functools.partial(mask_kernel, m),
        out_shape=jax.ShapeDtypeStruct(matrices.shape[1:], matrices.dtype),
        in_specs=[hbm, hbm],
        out_specs=pl.BlockSpec(memory_space=pltpu.VMEM),
        scratch_shapes=[
            pltpu.VMEM(keep.shape[1:], keep.dtype),
            pltpu.VMEM((rows // BLOCK, units), jnp.float32),
            pltpu.SemaphoreType.DMA((parts + 1,)),
        ],
        compiler_params=pltpu.CompilerParams(vmem_limit_bytes=10 << 20),
        cost_estimate=pl.CostEstimate(flops=0, bytes_accessed=cost, transcendentals=0),
        name="mask_matrix",
    )(*(pltpu.with_memory_space_constraint(a, pltpu.HBM) for a in (keep, matrices)))


def join_kernel(starts, *refs):
    *piece_refs, out_ref = refs
    width = out_ref.shape[1]
    for k, (start, piece_ref) in enumerate(zip(starts, piece_refs)):
        have = min(width, piece_ref.shape[1])
        out_ref[PAIR * k : PAIR * (k + 1), :have] = piece_ref[start : start + PAIR, :have]
        if have < width:
            out_ref[PAIR * k : PAIR * (k + 1), have:] = jnp.zeros((PAIR, width - have), out_ref.dtype)


def join(width, *pieces, cost=0):
    pieces = [p if isinstance(p, tuple) else (p, 0) for p in pieces]
    vmem = pl.BlockSpec(memory_space=pltpu.VMEM)
    return pl.pallas_call(
        functools.partial(join_kernel, [start for _, start in pieces]),
        out_shape=jax.ShapeDtypeStruct((PAIR * len(pieces), width), pieces[0][0].dtype),
        in_specs=[vmem] * len(pieces),
        out_specs=vmem,
        compiler_params=pltpu.CompilerParams(vmem_limit_bytes=4 << 20),
        cost_estimate=pl.CostEstimate(flops=0, bytes_accessed=cost, transcendentals=0),
        name="join",
    )(*(array for array, _ in pieces))


def project_kernel(where, last, place, gate_ref, up_ref, *refs):
    count = 1 + max(i for i, _ in where)
    pieces, refs = refs[:count], refs[count:]
    if last:
        total_ref, scale_ref, out_ref, x_ref = refs
    else:
        total_ref, scale_ref, x_ref = refs
    chip = place[0] // 2
    width = x_ref.shape[1]
    for k, (i, row) in enumerate(where):
        at = pl.multiple_of(PAIR * (chip ^ k), PAIR)
        x_ref[pl.ds(at, PAIR), :] = pieces[i][row : row + PAIR, :width]
        if not last:
            scale_ref[pl.ds(at, PAIR), :] = pieces[i][row : row + PAIR, width:].astype(jnp.float32)
    share = 1 - place[1] if last else place[1]
    span = pl.ds(pl.multiple_of(share * width, BLOCK), width)
    totals = [jnp.dot(x_ref[...], ref[span, :], preferred_element_type=jnp.float32) for ref in (gate_ref, up_ref)]
    if last:
        gate, up = (total_ref[m] + totals[m] for m in range(2))
        out_ref[0] = (scale_ref[:, :1] * (gate / (1.0 + jnp.exp(-gate))) * up).astype(out_ref.dtype)
    else:
        for m in range(2):
            total_ref[m] = totals[m]


def project(place, matrices, pieces, where, width, total=None, scale=None):
    last = total is not None
    units = matrices[0].shape[1]
    slots = PAIR * len(where)
    vmem = pl.BlockSpec(memory_space=pltpu.VMEM)
    args = [place, *matrices, *pieces]
    if last:
        args += [total, scale]
        out_shape = jax.ShapeDtypeStruct((1, slots, units), jnp.bfloat16)
    else:
        out_shape = [
            jax.ShapeDtypeStruct((2, slots, units), jnp.float32),
            jax.ShapeDtypeStruct((slots, LANES), jnp.float32),
        ]
    return pl.pallas_call(
        functools.partial(project_kernel, where, last),
        out_shape=out_shape,
        in_specs=[pl.BlockSpec(memory_space=pltpu.SMEM)] + [vmem] * (len(args) - 1),
        out_specs=vmem if last else [vmem, vmem],
        scratch_shapes=[pltpu.VMEM((slots, width), jnp.bfloat16)],
        compiler_params=pltpu.CompilerParams(vmem_limit_bytes=24 << 20),
        cost_estimate=pl.CostEstimate(
            flops=4 * slots * width * units, bytes_accessed=4 * width * units, transcendentals=slots * units
        ),
        name="project_last" if last else "project_first",
    )(*args)


def paired_form(tokens, route_ids, route_weight, gate_up, block_keep):
    n = lax.axis_size("expert")
    groups = n // 2
    me = lax.axis_index("expert")
    place = jnp.stack([me, lax.axis_index("tensor")]).astype(jnp.int32)
    width = tokens.shape[1]

    def move(a, shift):
        return lax.ppermute(a, "expert", [(s, s ^ shift) for s in range(n)])

    def cross(a):
        return lax.ppermute(a, "tensor", [(0, 1), (1, 0)])

    def after(a, *done):
        return lax.optimization_barrier((a, done))[0]

    ids, wgt = route_ids.T, route_weight.T
    partner = [move(a, 1) for a in (ids, wgt, tokens)]
    piece = list(dispatch(place, ids, wgt, tokens, partner, groups))
    keep = jnp.swapaxes(block_keep[0], 1, 2)
    got = [piece[0]] + [None] * (groups - 1)
    got[1] = move(piece[1], 2)
    block0 = cross(join(width, got[0], piece[2], cost=10 << 20))
    got[3] = move(piece[3], 6)
    got[7] = move(piece[7], 14)
    got[4] = move(piece[4], 8)
    got[2] = move(join(width + LANES, piece[2], (block0, 16), cost=10 << 20), 4)
    gate = mask_matrix(after(keep, piece[0], got[1]), gate_up[0], 0, cost=30 << 20)
    got[6] = move(after(piece[6], got[3]), 12)
    block4 = cross(join(width, got[6], cost=10 << 20))
    block1 = cross(join(width, got[1], got[3]))
    got[5] = move(after(piece[5], got[4]), 10)
    block2 = cross(join(width, got[4], got[7], cost=10 << 20))
    up = mask_matrix(after(keep, piece[0], got[4]), gate_up[0], 1, cost=30 << 20)
    block3 = cross(join(width, after(got[5], up), cost=10 << 20))
    masked = (gate, up)
    total, scale = project(place, masked, got, [(k, 0) for k in range(groups)], width)
    where = [(0, 0), (1, 0), (5, 16), (1, 16), (2, 0), (3, 0), (4, 0), (2, 16)]
    return project(place, masked, [block0, block1, block2, block3, block4, got[2]], where, width, total, scale)


def solution(mesh):
    paired = mesh.shape["tensor"] == 2 and mesh.shape["expert"] == 2 * PIECES
    return jax.shard_map(
        paired_form if paired else gathered_form,
        mesh=mesh,
        in_specs=(
            P("expert", "tensor"),
            P("expert", None),
            P("expert", None),
            P("expert", None, None, "tensor"),
            P("expert", None, None, "tensor"),
        ),
        out_specs=P("expert", None, "tensor"),
        check_vma=False,
    )
```
